512 devices in a mesh: row: 16 (over y, core), col: 32 (over x, z).
Axes of the slice: x: 4, y: 8, z: 8, core: 2. Of those that a mesh axis runs over, the one named last changes fastest.
Arguments:
- matrix: float32 [16384, 16384], P('row', 'col'), may hold values from -4 to 4, as said below
- panel: float32 [16384, 64], P('row'), may hold values from -1200 to 1200
Outputs:
- updated: float32 [16384, 16384], P('row', 'col')
- w_rows: float32 [16384, 64], P('row')
- basis: float32 [16384, 64], P('row')
The draws below stay inside these ranges and needn't reach their ends.
Inputs may be any that keep to these rules, and one draw needn't show every extreme that they name: Read in global order (both indices mapped back through their cyclic orders) the matrix is exactly symmetric.
All inputs are finite; a program needn't handle non-finite values.
Results may differ from the reference program's by a relative error of at most 0.00007.
Values sent between devices are 32-bit elements; how exact they have to be, the bound alone decides.
A program may use at most 64 MiB of HBM per device.

```python
import math
import jax
import jax.numpy as jnp
from jax import lax

NB = 64
M = 16384
N_ROW = 16
N_COL = 32


def draw_matrix(key, part):
    key = jax.random.fold_in(key, 11)
    first = jax.random.fold_in(key, 0)
    base = 0.5 * jnp.clip(jax.random.normal(first, (M, M), jnp.float32), -4.0, 4.0)
    row_ids = jnp.arange(M)[:, None]
    col_ids = jnp.arange(M)[None, :]
    sym = jnp.where(row_ids >= col_ids, base, base.T)
    row_blocks = M // (NB * N_ROW)
    col_blocks = M // (NB * N_COL)
    sym = sym.reshape(row_blocks, N_ROW, NB, M).transpose(1, 0, 2, 3).reshape(M, M)
    sym = sym.reshape(M, col_blocks, N_COL, NB).transpose(0, 2, 1, 3).reshape(M, M)
    return sym


def draw_panel(key, part):
    key = jax.random.fold_in(key, 12)
    first, second, third = jax.random.split(key, 3)
    base = jnp.clip(jax.random.normal(first, (M, NB), jnp.float32), -4.0, 4.0)
    col_scale = jnp.exp(jax.random.uniform(second, (NB,), jnp.float32, 0.0, math.log(10.0)))
    row_scale = jnp.exp(jax.random.uniform(third, (M,), jnp.float32, 0.0, math.log(10.0)))
    ramp = 1.0 + 2.0 * jnp.arange(M, dtype=jnp.float32) / M
    return base * col_scale[None, :] * (row_scale * ramp)[:, None]


def setup_inputs(seed: int = 0) -> dict:
    keys = jax.random.split(jax.random.key(seed), 3)
    matrix = draw_matrix(jax.random.fold_in(keys[2], 71), 0)
    panel = draw_panel(jax.random.fold_in(keys[2], 71), 0)
    return dict(matrix=matrix, panel=panel)


HIGH = lax.Precision.HIGHEST

def to_global(values, parts):
    total = values.shape[0]
    blocks = total // (NB * parts)
    return values.reshape(parts, blocks, NB, -1).transpose(1, 0, 2, 3).reshape(total, -1)

def to_stored(values, parts):
    total = values.shape[0]
    blocks = total // (NB * parts)
    return values.reshape(blocks, parts, NB, -1).transpose(1, 0, 2, 3).reshape(total, -1)

def reference(matrix, panel):
    gram = jnp.dot(panel.T.astype(jnp.float32), panel.astype(jnp.float32), precision=HIGH, preferred_element_type=jnp.float32)
    lower = lax.linalg.cholesky(gram)
    basis = lax.linalg.triangular_solve(lower, panel, left_side=False, lower=True, transpose_a=True)
    basis_cols = to_stored(to_global(basis, N_ROW), N_COL)
    product = jnp.dot(matrix.astype(jnp.float32), basis_cols.astype(jnp.float32), precision=HIGH, preferred_element_type=jnp.float32)
    correction = jnp.dot(basis.T.astype(jnp.float32), product.astype(jnp.float32), precision=HIGH, preferred_element_type=jnp.float32)
    w_rows = 2.0 * (product - jnp.dot(basis.astype(jnp.float32), correction.astype(jnp.float32), precision=HIGH, preferred_element_type=jnp.float32))
    w_cols = to_stored(to_global(w_rows, N_ROW), N_COL)
    left = jnp.concatenate([basis, w_rows], axis=1)
    right = jnp.concatenate([w_cols, basis_cols], axis=1)
    updated = matrix - jnp.dot(left.astype(jnp.float32), right.T.astype(jnp.float32), precision=HIGH, preferred_element_type=jnp.float32)
    return (updated, w_rows, basis)
```

```python
import functools

import jax
import jax.numpy as jnp
from jax import lax
from jax.experimental import pallas as pl
from jax.experimental.pallas import tpu as pltpu
from jax.sharding import PartitionSpec as P

MESH = pl.DeviceIdType.MESH
HIGH = lax.Precision.HIGHEST
F32 = jnp.float32


def dot(left, right, dims=((1,), (0,))):
    return lax.dot_general(left, right, (dims, ((), ())), precision=HIGH, preferred_element_type=F32)


def whole(ref, lead):
    rows = []
    for y in range(8):
        rows.append(jnp.concatenate([ref[lead + (2 * y,)], ref[lead + (2 * y + 1,)]], axis=1))
    return jnp.concatenate(rows, axis=0)


def eliminate(aug, first, last):
    ids = lax.broadcasted_iota(jnp.int32, (64, 1), 0)
    for j in range(first, last):
        row = aug[j : j + 1, :]
        factor = aug[:, j : j + 1] * (1.0 / row[:, j : j + 1])
        aug = aug - jnp.where(ids > j, factor, 0.0) * row
    return aug


def exchange(
    mat, pan, v_out, w_out, right_out,
    gsend, grecv, psend, precv, xsend, xrecv, piece, acol, arow, tsend, trecv, usend, urecv,
    ssem, rsem,
):
    r, c = lax.axis_index("row"), lax.axis_index("col")
    y, core, x, z = r // 2, r % 2, c // 8, c % 8
    half, root = c // 16, c % 16

    def put(src, dst, k, row, col):
        pltpu.make_async_remote_copy(
            src_ref=src, dst_ref=dst, send_sem=ssem.at[k], recv_sem=rsem.at[k],
            device_id={"row": row, "col": col}, device_id_type=MESH,
        ).start()

    def keep(src, dst, k):
        pltpu.make_async_copy(src, dst, rsem.at[k]).start()

    def got(ref, k):
        pltpu.make_async_copy(ref, ref, rsem.at[k]).wait()

    def sent(ref, k):
        pltpu.make_async_copy(ref, ref, ssem.at[k]).wait()

    def loop(first, last, body):
        lax.fori_loop(first, last, lambda i, s: (body(i), s)[1], 0)

    mine = jnp.concatenate(
        [pan[pl.ds(pl.multiple_of(128 * k + 64 * half, 64), 64), :] for k in range(8)], axis=0
    )
    psend[...] = mine.T

    @pl.when(root == r)
    def _():
        keep(psend, precv, 0)

    @pl.when(root != r)
    def _():
        put(psend, precv, 0, root, r + 16 * half)

    pant = pan[...].T
    gram = dot(pant, pan[...])
    gsend[...] = jnp.concatenate([gram[:32], gram[32:]], axis=1)
    keep(gsend, grecv.at[r], 1)
    loop(1, 16, lambda i: put(gsend, grecv.at[r], 1, (r + i) % 16, c))

    prod = dot(pant, mat[...])
    for k in range(16):
        xsend[k] = prod[8 * (k // 2) : 8 * (k // 2) + 8, 256 * (k % 2) : 256 * (k % 2) + 256]
    keep(xsend.at[r], xrecv.at[r], 2)

    def scatter(i):
        d = (r + i) % 16
        put(xsend.at[d], xrecv.at[r], 2, d, c)

    loop(1, 16, scatter)
    got(xrecv, 2)
    total = xrecv[0]
    for k in range(1, 16):
        total = total + xrecv[k]
    piece[...] = total

    got(precv, 0)
    tpart = dot(total, precv[:, pl.ds(pl.multiple_of(256 * core, 256), 256)], ((1,), (1,)))
    tsend[...] = jnp.concatenate([tpart, tpart], axis=1)
    me = z * 2 + core
    keep(tsend, trecv.at[me], 3)

    def share(i):
        d = (me + i) % 16
        put(tsend, trecv.at[me], 3, y * 2 + d % 2, x * 8 + d // 2)

    loop(1, 16, share)

    loop(1, 32, lambda i: put(piece, arow.at[half, r], 4, root, (c + i) % 32))

    @pl.when(root == r)
    def _():
        keep(piece, arow.at[half, r], 4)

    @pl.when(root != r)
    def _():
        put(piece, arow.at[half, r], 4, root, c)

    keep(piece, acol.at[r], 5)
    loop(1, 16, lambda i: put(piece, acol.at[r], 5, (r + i) % 16, c))

    got(grecv, 1)
    packed = grecv[0]
    for k in range(1, 16):
        packed = packed + grecv[k]
    gram = jnp.concatenate([packed[:, :64], packed[:, 64:]], axis=0)
    eye = (
        lax.broadcasted_iota(jnp.int32, (64, 64), 0) == lax.broadcasted_iota(jnp.int32, (64, 64), 1)
    ).astype(F32)
    aug = eliminate(jnp.concatenate([gram, eye], axis=1), 0, 24)

    got(trecv, 3)
    total = trecv[0]
    for k in range(1, 16):
        total = total + trecv[k]
    usend[...] = total
    place = x * 8 + y
    keep(usend, urecv.at[place], 6)

    def share2(i):
        d = (place + i) % 32
        put(usend, urecv.at[place], 6, (d % 8) * 2 + core, (d // 8) * 8 + z)

    loop(1, 32, share2)

    aug = eliminate(aug, 24, 64)
    diag = jnp.sum(aug[:, :64] * eye, axis=1, keepdims=True)
    linv = aug[:, 64:] * lax.rsqrt(diag)

    v_rows = dot(pan[...], linv, ((1,), (1,)))
    v_out[...] = v_rows
    v_cols = dot(linv, precv[...])

    got(acol, 5)
    av_cols = dot(linv, whole(acol, ()))
    got(arow, 4)
    av_rows = [dot(linv, whole(arow, (h,))).T for h in range(2)]
    av_rows = jnp.concatenate(
        [av_rows[h][64 * k : 64 * k + 64] for k in range(8) for h in range(2)], axis=0
    )

    got(urecv, 6)
    rows = []
    for k in range(8):
        rows.append(urecv[k] + urecv[8 + k] + urecv[16 + k] + urecv[24 + k])
    corr = 2.0 * dot(dot(linv, jnp.concatenate(rows, axis=0)[:, :64]), linv, ((1,), (1,)))
    w_out[...] = 2.0 * av_rows - dot(v_rows, corr)
    right_out[:64] = 2.0 * av_cols - dot(corr, v_cols, ((0,), (0,)))
    right_out[64:] = v_cols

    @pl.when(root != r)
    def _():
        sent(psend, 0)
        sent(arow, 4)

    @pl.when(root == r)
    def _():
        sent(arow.at[0], 4)
        sent(arow.at[1, pl.ds(0, 15)], 4)

    sent(grecv.at[pl.ds(0, 15)], 1)
    sent(xrecv.at[pl.ds(0, 15)], 2)
    sent(trecv.at[pl.ds(0, 15)], 3)
    sent(acol.at[pl.ds(0, 15)], 5)
    sent(urecv.at[pl.ds(0, 31)], 6)


def update(mat, v_rows, w_rows, right, out, w_out, v_out):
    left = jnp.concatenate([v_rows[...], w_rows[...]], axis=1)
    out[...] = mat[...] - dot(left, right[...])
    w_out[...] = w_rows[...]
    v_out[...] = v_rows[...]


def local(mat, pan):
    vmem = pl.BlockSpec(memory_space=pltpu.VMEM)
    v_rows, w_rows, right = pl.pallas_call(
        exchange,
        out_shape=[
            jax.ShapeDtypeStruct((1024, 64), F32),
            jax.ShapeDtypeStruct((1024, 64), F32),
            jax.ShapeDtypeStruct((128, 512), F32),
        ],
        in_specs=[vmem, vmem],
        out_specs=[vmem] * 3,
        scratch_shapes=[
            pltpu.VMEM((32, 128), F32),
            pltpu.VMEM((16, 32, 128), F32),
            pltpu.VMEM((64, 512), F32),
            pltpu.VMEM((64, 512), F32),
            pltpu.VMEM((16, 8, 256), F32),
            pltpu.VMEM((16, 8, 256), F32),
            pltpu.VMEM((8, 256), F32),
            pltpu.VMEM((16, 8, 256), F32),
            pltpu.VMEM((2, 16, 8, 256), F32),
            pltpu.VMEM((8, 128), F32),
            pltpu.VMEM((16, 8, 128), F32),
            pltpu.VMEM((8, 128), F32),
            pltpu.VMEM((32, 8, 128), F32),
            pltpu.SemaphoreType.DMA((7,)),
            pltpu.SemaphoreType.DMA((7,)),
        ],
        compiler_params=pltpu.CompilerParams(has_side_effects=True, vmem_limit_bytes=48 * 1024 * 1024),
    )(mat, pan)
    steps, rows = 8, 128
    by_row = lambda width: pl.BlockSpec((rows, width), lambda i: (i, 0))
    return pl.pallas_call(
        update,
        grid=(steps,),
        out_shape=[
            jax.ShapeDtypeStruct((1024, 512), F32),
            jax.ShapeDtypeStruct((1024, 64), F32),
            jax.ShapeDtypeStruct((1024, 64), F32),
        ],
        in_specs=[by_row(512), by_row(64), by_row(64), pl.BlockSpec((128, 512), lambda i: (0, 0))],
        out_specs=[by_row(512), by_row(64), by_row(64)],
        compiler_params=pltpu.CompilerParams(vmem_limit_bytes=32 * 1024 * 1024),
    )(mat, v_rows, w_rows, right)


def solution(mesh):
    return jax.shard_map(
        local,
        mesh=mesh,
        in_specs=(P("row", "col"), P("row", None)),
        out_specs=(P("row", "col"), P("row", None), P("row", None)),
        check_vma=False,
    )
```

```python
import jax
import jax.numpy as jnp
from jax import lax
from jax.experimental import pallas as pl
from jax.experimental.pallas import tpu as pltpu
from jax.sharding import PartitionSpec as P

VLIM = 40
SPACE = pltpu.HBM
CUT1 = 0
CUT2 = 24
ROWS = 256
MESH = pl.DeviceIdType.MESH
HIGH = lax.Precision.HIGHEST
F32 = jnp.float32
BF16 = jnp.bfloat16


def dot(left, right, dims=((1,), (0,))):
    return lax.dot_general(left, right, (dims, ((), ())), precision=HIGH, preferred_element_type=F32)


def split(value):
    high = value.astype(BF16)
    return high, (value - high.astype(F32)).astype(BF16)


def whole(ref, lead):
    rows = []
    for y in range(8):
        rows.append(jnp.concatenate([ref[lead + (2 * y,)], ref[lead + (2 * y + 1,)]], axis=1))
    return jnp.concatenate(rows, axis=0)


def eliminate(aug, first, last):
    ids = lax.broadcasted_iota(jnp.int32, (64, 1), 0)
    for j in range(first, last):
        row = aug[j : j + 1, :]
        factor = aug[:, j : j + 1] * (1.0 / row[:, j : j + 1])
        aug = aug - jnp.where(ids > j, factor, 0.0) * row
    return aug


def exchange(
    mat_hbm, pan_hbm, out,
    mat, pan, gsend, grecv, qsend, gall, psend, precv, xsend, xrecv, piece, moved, acol, arow,
    tsend, trecv, usend, urecv,
    ssem, rsem, msem,
):
    r, c = lax.axis_index("row"), lax.axis_index("col")
    y, core, x, z = r // 2, r % 2, c // 8, c % 8
    drains = []

    def put(src, dst, k, row, col, recv=None):
        pltpu.make_async_remote_copy(
            src_ref=src, dst_ref=dst, send_sem=ssem.at[k], recv_sem=rsem.at[k if recv is None else recv],
            device_id={"row": row, "col": col}, device_id_type=MESH,
        ).start()

    def keep(src, dst, k):
        pltpu.make_async_copy(src, dst, rsem.at[k]).start()

    def got(ref, k):
        pltpu.make_async_copy(ref, ref, rsem.at[k]).wait()

    def sent(ref, k):
        drains.append(lambda: pltpu.make_async_copy(ref, ref, ssem.at[k]).wait())

    def loop(first, last, body):
        lax.fori_loop(first, last, lambda i, s: (body(i), s)[1], 0)

    def finish():
        for drain in drains:
            drain()

    barrier = pltpu.get_barrier_semaphore()

    def greet(row, col):
        pl.semaphore_signal(barrier, inc=1, device_id={"row": row, "col": col}, device_id_type=MESH)

    load = pltpu.make_async_copy(mat_hbm, mat, msem.at[0])
    load.start()
    load_pan = pltpu.make_async_copy(pan_hbm, pan, msem.at[1])
    load_pan.start()

    core_to = (x - r // 8) % 2
    x_to = (x - core_to) % 4
    y_to = (z - r % 8 + y + 4) % 8
    half_to = x_to // 2
    row_to, col_to = 2 * y_to + core_to, 8 * x_to + r % 8
    row_up, col_up = c % 16, 8 * ((x + core) % 4) + (z + y - (c % 16) // 2 + 4) % 8
    greet(row_to, col_to)
    greet(row_up, col_up)
    loop(1, 16, lambda i: greet((r + i) % 16, c))
    loop(1, 8, lambda i: greet(r, 8 * x + (z + i) % 8))
    loop(1, 4, lambda i: greet(r, 8 * ((x + i) % 4) + z))

    load_pan.wait()
    for k in range(4):
        low, high = pan[:, 256 * k : 256 * k + 128], pan[:, 256 * k + 128 : 256 * k + 256]
        psend[k // 2, :, 128 * (k % 2) : 128 * (k % 2) + 128] = jnp.where(
            half_to == 0,
            jnp.concatenate([low[:, :64], high[:, :64]], axis=1),
            jnp.concatenate([low[:, 64:], high[:, 64:]], axis=1),
        )
    pant = pan[...]
    gram = dot(pant, pant, ((1,), (1,)))
    gsend[...] = jnp.concatenate([gram[:32], gram[32:]], axis=1)
    load.wait()
    ph, pl_ = split(pant)
    ah, al = split(mat[...])
    both = jnp.dot(jnp.concatenate([ph, pl_], axis=0), ah, preferred_element_type=F32)
    prod = both[:64] + (both[64:] + jnp.dot(ph, al, preferred_element_type=F32))
    for k in range(16):
        xsend[k] = prod[8 * (k // 2) : 8 * (k // 2) + 8, 256 * (k % 2) : 256 * (k % 2) + 256]

    pl.semaphore_wait(barrier, 27)
    put(psend.at[core_to], precv.at[core_to], 0, row_to, col_to)

    def scatter(i):
        d = (r + 8 + i) % 16

        @pl.when(i != 8)
        def _():
            put(xsend.at[d], xrecv.at[r], 3, d, c)

    loop(0, 16, scatter)
    keep(xsend.at[r], xrecv.at[r], 3)
    share = gsend.at[pl.ds(pl.multiple_of(8 * x, 8), 8)]
    loop(1, 16, lambda i: put(share, grecv.at[r], 2, (r + i) % 16, c))
    keep(share, grecv.at[r], 2)
    put(psend.at[1 - core_to], precv.at[1 - core_to], 1, row_to, col_to)
    sent(psend.at[0], 0)
    sent(xrecv.at[pl.ds(0, 15)], 3)
    sent(grecv.at[pl.ds(0, 15)], 2)
    sent(psend.at[0], 1)
    got(xrecv, 3)
    total = xrecv[0]
    for k in range(1, 16):
        total = total + xrecv[k]
    piece[...] = total
    put(piece, moved, 4, row_up, col_up)
    sent(piece, 4)

    got(precv.at[core], 0)
    tpart = dot(total, precv[core], ((1,), (1,)))
    tsend[...] = jnp.concatenate([tpart[:4], tpart[4:]], axis=1)
    me = 2 * z + core

    def share_z(i):
        d = (me + i) % 16
        put(tsend, trecv.at[me], 5, 2 * y + d % 2, 8 * x + d // 2)

    loop(1, 16, share_z)
    keep(tsend, trecv.at[me], 5)
    sent(trecv.at[pl.ds(0, 15)], 5)

    got(grecv, 2)
    quarter = grecv[0]
    for k in range(1, 16):
        quarter = quarter + grecv[k]
    qsend[...] = quarter
    loop(1, 4, lambda i: put(qsend, gall.at[x], 8, r, 8 * ((x + i) % 4) + z))
    keep(qsend, gall.at[x], 8)
    sent(gall.at[pl.ds(0, 3)], 8)

    loop(1, 16, lambda i: put(piece, acol.at[r], 6, (r + i) % 16, c))
    keep(piece, acol.at[r], 6)
    sent(acol.at[pl.ds(0, 15)], 6)

    got(gall, 8)
    packed = jnp.concatenate([gall[k] for k in range(4)], axis=0)
    gram = jnp.concatenate([packed[:, :64], packed[:, 64:]], axis=0)
    eye = (
        lax.broadcasted_iota(jnp.int32, (64, 64), 0) == lax.broadcasted_iota(jnp.int32, (64, 64), 1)
    ).astype(F32)
    aug = jnp.concatenate([gram, eye], axis=1)
    aug = eliminate(aug, 0, CUT1)

    got(moved, 4)
    loop(1, 32, lambda i: put(moved, arow.at[half_to, row_to], 9, r, (c + i) % 32))
    keep(moved, arow.at[half_to, row_to], 9)
    sent(arow.at[0, pl.ds(0, 15)], 9)
    sent(arow.at[1], 9)

    aug = eliminate(aug, CUT1, CUT2)
    got(trecv, 5)
    total = trecv[0]
    for k in range(1, 16):
        total = total + trecv[k]
    usend[...] = total
    place = 8 * x + y

    def share_xy(i):
        d = (place + i) % 32
        put(usend, urecv.at[place], 7, 2 * (d % 8) + core, 8 * (d // 8) + z)

    loop(1, 32, share_xy)
    keep(usend, urecv.at[place], 7)
    sent(urecv.at[pl.ds(0, 31)], 7)
    aug = eliminate(aug, CUT2, 64)
    diag = jnp.sum(aug[:, :64] * eye, axis=1, keepdims=True)
    linv = aug[:, 64:] * lax.rsqrt(diag)

    v_rows = dot(linv, pant)
    out[:, :1024] = v_rows
    got(precv.at[0], 1)
    v_cols = dot(linv, jnp.concatenate([precv[0], precv[1]], axis=1))
    out[:, 2048:2560] = v_cols
    got(acol, 6)
    av_cols = dot(linv, whole(acol, ()))

    got(arow, 9)
    even, odd = whole(arow, (0,)), whole(arow, (1,))
    blocks = []
    for k in range(8):
        blocks += [even[:, 64 * k : 64 * k + 64], odd[:, 64 * k : 64 * k + 64]]
    av_rows = dot(linv, jnp.concatenate(blocks, axis=1))

    got(urecv, 7)
    rows = []
    for k in range(8):
        pair = (urecv[k] + urecv[8 + k]) + (urecv[16 + k] + urecv[24 + k])
        rows += [pair[:, :64], pair[:, 64:]]
    corr = 2.0 * dot(dot(linv, jnp.concatenate(rows, axis=0)), linv, ((1,), (1,)))
    out[:, 1024:2048] = 2.0 * av_rows - dot(corr, v_rows, ((0,), (0,)))
    out[:, 2560:] = 2.0 * av_cols - dot(corr, v_cols, ((0,), (0,)))
    finish()


def update(mat, parts, out, w_out, v_out):
    step = pl.program_id(0)
    first = pl.multiple_of(ROWS * step, ROWS)
    v_rows, w_rows = parts[:, pl.ds(first, ROWS)], parts[:, pl.ds(1024 + first, ROWS)]
    lh, ll = split(jnp.concatenate([v_rows, w_rows], axis=0).T)
    rh, rl = split(jnp.concatenate([parts[:, 2560:], parts[:, 2048:2560]], axis=0))
    out[...] = mat[...] - jnp.dot(
        jnp.concatenate([lh, lh, ll], axis=1), jnp.concatenate([rh, rl, rh], axis=0),
        preferred_element_type=F32,
    )
    w_out[...] = w_rows
    v_out[...] = v_rows


def local(mat, pan):
    vmem = pl.BlockSpec(memory_space=pltpu.VMEM)
    parts = pl.pallas_call(
        exchange,
        out_shape=jax.ShapeDtypeStruct((64, 3072), F32),
        in_specs=[pl.BlockSpec(memory_space=SPACE)] * 2,
        out_specs=vmem,
        scratch_shapes=[
            pltpu.VMEM((1024, 512), F32),
            pltpu.VMEM((64, 1024), F32),
            pltpu.VMEM((32, 128), F32),
            pltpu.VMEM((16, 8, 128), F32),
            pltpu.VMEM((8, 128), F32),
            pltpu.VMEM((4, 8, 128), F32),
            pltpu.VMEM((2, 64, 256), F32),
            pltpu.VMEM((2, 64, 256), F32),
            pltpu.VMEM((16, 8, 256), F32),
            pltpu.VMEM((16, 8, 256), F32),
            pltpu.VMEM((8, 256), F32),
            pltpu.VMEM((8, 256), F32),
            pltpu.VMEM((16, 8, 256), F32),
            pltpu.VMEM((2, 16, 8, 256), F32),
            pltpu.VMEM((4, 128), F32),
            pltpu.VMEM((16, 4, 128), F32),
            pltpu.VMEM((4, 128), F32),
            pltpu.VMEM((32, 4, 128), F32),
            pltpu.SemaphoreType.DMA((10,)),
            pltpu.SemaphoreType.DMA((10,)),
            pltpu.SemaphoreType.DMA((2,)),
        ],
        compiler_params=pltpu.CompilerParams(
            has_side_effects=True, collective_id=0, vmem_limit_bytes=VLIM * 1024 * 1024
        ),
    )(mat, pan.T)
    across = pl.BlockSpec((64, ROWS), lambda i: (0, i))
    down = pl.BlockSpec((ROWS, 512), lambda i: (i, 0))
    updated, w_rows, v_rows = pl.pallas_call(
        update,
        grid=(1024 // ROWS,),
        out_shape=[
            jax.ShapeDtypeStruct((1024, 512), F32),
            jax.ShapeDtypeStruct((64, 1024), F32),
            jax.ShapeDtypeStruct((64, 1024), F32),
        ],
        in_specs=[down, pl.BlockSpec((64, 3072), lambda i: (0, 0))],
        out_specs=[down, across, across],
        compiler_params=pltpu.CompilerParams(vmem_limit_bytes=32 * 1024 * 1024),
    )(mat, parts)
    return updated, w_rows.T, v_rows.T


def solution(mesh):
    return jax.shard_map(
        local,
        mesh=mesh,
        in_specs=(P("row", "col"), P("row", None)),
        out_specs=(P("row", "col"), P("row", None), P("row", None)),
        check_vma=False,
    )
```

```python
import jax
import jax.numpy as jnp
from jax import lax
from jax.experimental import pallas as pl
from jax.experimental.pallas import tpu as pltpu
from jax.sharding import PartitionSpec as P

MESH = pl.DeviceIdType.MESH
HIGH = lax.Precision.HIGHEST
F32 = jnp.float32
BF16 = jnp.bfloat16


def dot(left, right, dims=((1,), (0,))):
    return lax.dot_general(left, right, (dims, ((), ())), precision=HIGH, preferred_element_type=F32)


def split(value):
    high = value.astype(BF16)
    return high, (value - high.astype(F32)).astype(BF16)


def dot3(left, right, dims=((1,), (0,))):
    lh, ll = split(left)
    rh, rl = split(right)

    def one(u, v):
        return lax.dot_general(u, v, (dims, ((), ())), preferred_element_type=F32)

    return one(lh, rh) + (one(lh, rl) + one(ll, rh))


def whole(piece):
    return jnp.concatenate(
        [jnp.concatenate([piece(y, 0), piece(y, 1)], axis=1) for y in range(8)], axis=0
    )


def lower_inverse(gram):
    size = gram.shape[0]
    ids = lax.broadcasted_iota(jnp.int32, (size, 1), 0)
    eye = (
        lax.broadcasted_iota(jnp.int32, (size, size), 0)
        == lax.broadcasted_iota(jnp.int32, (size, size), 1)
    ).astype(F32)
    aug = jnp.concatenate([gram, eye], axis=1)
    for j in range(size):
        row = aug[j : j + 1, :]
        factor = aug[:, j : j + 1] * (1.0 / row[:, j : j + 1])
        aug = aug - jnp.where(ids > j, factor, 0.0) * row
    diag = jnp.sum(aug[:, :size] * eye, axis=1, keepdims=True)
    return aug[:, size:] * lax.rsqrt(diag)


def exchange(
    mat_hbm, pan_hbm, out,
    mat, pan, gsend, grecv, qsend, gall, psend, precv, xsend, xrecv, piece, moved, acol, arow,
    tsend, trecv, usend, urecv,
    ssem, rsem, msem, heard,
):
    r, c = lax.axis_index("row"), lax.axis_index("col")
    y, core, x, z = r // 2, r % 2, c // 8, c % 8
    drains = []

    def put(src, dst, k, row, col, recv=None):
        pltpu.make_async_remote_copy(
            src_ref=src, dst_ref=dst, send_sem=ssem.at[k], recv_sem=rsem.at[k if recv is None else recv],
            device_id={"row": row, "col": col}, device_id_type=MESH,
        ).start()

    def keep(src, dst, k):
        pltpu.make_async_copy(src, dst, rsem.at[k]).start()

    def got(ref, k):
        pltpu.make_async_copy(ref, ref, rsem.at[k]).wait()

    def sent(ref, k):
        drains.append(lambda: pltpu.make_async_copy(ref, ref, ssem.at[k]).wait())

    def loop(first, last, body):
        lax.fori_loop(first, last, lambda i, s: (body(i), s)[1], 0)

    def finish():
        for drain in drains:
            drain()

    barrier = pltpu.get_barrier_semaphore()

    def greet(row, col):
        pl.semaphore_signal(barrier, inc=1, device_id={"row": row, "col": col}, device_id_type=MESH)

    load = pltpu.make_async_copy(mat_hbm, mat, msem.at[0])
    load.start()
    load_pan = pltpu.make_async_copy(pan_hbm, pan, msem.at[1])
    load_pan.start()

    core_to = (x - r // 8) % 2
    x_to = (x - core_to) % 4
    y_to = (z - r % 8 + y + 4) % 8
    half_to = x_to // 2
    row_to, col_to = 2 * y_to + core_to, 8 * x_to + r % 8
    row_up, col_up = c % 16, 8 * ((x + core) % 4) + (z + y - (c % 16) // 2 + 4) % 8
    greet(row_to, col_to)
    greet(row_up, col_up)
    loop(1, 16, lambda i: greet((r + i) % 16, c))
    loop(1, 8, lambda i: greet(r, 8 * x + (z + i) % 8))
    loop(1, 4, lambda i: greet(r, 8 * ((x + i) % 4) + z))

    load_pan.wait()
    for k in range(4):
        low, high = pan[:, 256 * k : 256 * k + 128], pan[:, 256 * k + 128 : 256 * k + 256]
        psend[k // 2, :, 128 * (k % 2) : 128 * (k % 2) + 128] = jnp.where(
            half_to == 0,
            jnp.concatenate([low[:, :64], high[:, :64]], axis=1),
            jnp.concatenate([low[:, 64:], high[:, 64:]], axis=1),
        )
    pant = pan[...]
    gram = dot(pant, pant, ((1,), (1,)))
    gsend[...] = jnp.concatenate([gram[:32], gram[32:]], axis=1)
    load.wait()
    ph, pl_ = split(pant)
    ah, al = split(mat[...])
    both = jnp.dot(jnp.concatenate([ph, pl_], axis=0), ah, preferred_element_type=F32)
    prod = both[:64] + (both[64:] + jnp.dot(ph, al, preferred_element_type=F32))
    for k in range(16):
        xsend[k] = prod[8 * (k // 2) : 8 * (k // 2) + 8, 256 * (k % 2) : 256 * (k % 2) + 256]

    pl.semaphore_wait(barrier, 27)
    put(psend.at[core_to], precv.at[core_to], 0, row_to, col_to)
    sent(psend.at[0], 0)

    def scatter(i):
        d = (r + i) % 16
        put(xsend.at[d], xrecv.at[r], 3, d, c)

    loop(1, 16, scatter)
    keep(xsend.at[r], xrecv.at[r], 3)
    sent(xrecv.at[pl.ds(0, 15)], 3)
    share = gsend.at[pl.ds(pl.multiple_of(8 * x, 8), 8)]
    loop(1, 16, lambda i: put(share, grecv.at[r], 2, (r + i) % 16, c))
    keep(share, grecv.at[r], 2)
    sent(grecv.at[pl.ds(0, 15)], 2)
    loop(1, 4, lambda i: pl.semaphore_signal(
        heard, inc=1, device_id={"row": r, "col": 8 * ((x + i) % 4) + z}, device_id_type=MESH
    ))
    got(xrecv, 3)
    total = xrecv[0]
    for k in range(1, 16):
        total = total + xrecv[k]
    piece[...] = total
    put(piece, moved, 4, row_up, col_up)
    sent(piece, 4)

    got(precv.at[core], 0)
    tpart = dot(total, precv[core], ((1,), (1,)))
    tsend[...] = jnp.concatenate([tpart[:4], tpart[4:]], axis=1)
    me = 2 * z + core

    def share_z(i):
        d = (me + i) % 16
        put(tsend, trecv.at[me], 5, 2 * y + d % 2, 8 * x + d // 2)

    loop(1, 16, share_z)
    keep(tsend, trecv.at[me], 5)
    sent(trecv.at[pl.ds(0, 15)], 5)
    put(precv.at[core], precv.at[core], 1, r + 1 - 2 * core, c)
    sent(precv.at[0], 1)

    got(grecv, 2)
    quarter = grecv[0]
    for k in range(1, 16):
        quarter = quarter + grecv[k]
    qsend[...] = quarter
    loop(1, 4, lambda i: put(qsend, gall.at[x], 8, r, 8 * ((x + i) % 4) + z))
    keep(qsend, gall.at[x], 8)
    sent(gall.at[pl.ds(0, 3)], 8)

    loop(1, 8, lambda i: put(piece, acol.at[core, y], 6, (r + 2 * i) % 16, c))
    keep(piece, acol.at[core, y], 6)
    sent(acol.at[0, pl.ds(0, 7)], 6)

    got(moved, 4)
    pl.semaphore_wait(heard, 3)

    def spread(i):
        d = 8 * (i % 4) + i // 4

        @pl.when(d != c)
        def _():
            put(moved, arow.at[half_to, row_to], 9, r, d)

    loop(0, 32, spread)
    keep(moved, arow.at[half_to, row_to], 9)
    sent(arow.at[0, pl.ds(0, 15)], 9)
    sent(arow.at[1], 9)

    got(trecv, 5)
    total = trecv[0]
    for k in range(1, 16):
        total = total + trecv[k]
    usend[...] = total
    place = 8 * x + y

    def share_xy(i):
        d = (place + i) % 32
        put(usend, urecv.at[place], 7, 2 * (d % 8) + core, 8 * (d // 8) + z)

    loop(1, 32, share_xy)
    keep(usend, urecv.at[place], 7)
    sent(urecv.at[pl.ds(0, 31)], 7)

    got(acol.at[core], 6)
    put(acol.at[core], acol.at[core], 10, r + 1 - 2 * core, c)
    sent(acol.at[0], 10)

    got(gall, 8)
    packed = jnp.concatenate([gall[k] for k in range(4)], axis=0)
    linv = lower_inverse(jnp.concatenate([packed[:, :64], packed[:, 64:]], axis=0))

    v_rows = dot(linv, pant)
    out[:, :1024] = v_rows
    got(precv.at[0], 1)
    v_cols = dot(linv, jnp.concatenate([precv[0], precv[1]], axis=1))
    out[:, 2048:2560] = v_cols
    got(acol.at[0], 10)
    double = 2.0 * linv
    w_cols = dot3(double, whole(lambda y, core: acol[core, y]))
    both = jnp.concatenate([v_rows, v_cols], axis=1)

    got(urecv, 7)
    rows = []
    for k in range(8):
        pair = (urecv[k] + urecv[8 + k]) + (urecv[16 + k] + urecv[24 + k])
        rows += [pair[:, :64], pair[:, 64:]]
    corr = dot3(dot3(double, jnp.concatenate(rows, axis=0)), linv, ((1,), (1,)))
    part = dot3(corr, both, ((0,), (0,)))

    got(arow, 9)
    even, odd = (whole(lambda y, core: arow[h, 2 * y + core]) for h in range(2))
    blocks = []
    for k in range(8):
        blocks += [even[:, 64 * k : 64 * k + 64], odd[:, 64 * k : 64 * k + 64]]
    w_rows = dot3(double, jnp.concatenate(blocks, axis=1))
    out[:, 1024:2048] = w_rows - part[:, :1024]
    out[:, 2560:] = w_cols - part[:, 1024:]
    finish()


def update(mat, parts, out, w_out, v_out):
    step = pl.program_id(0)
    first = pl.multiple_of(512 * step, 512)
    v_rows, w_rows = parts[:, pl.ds(first, 512)], parts[:, pl.ds(1024 + first, 512)]
    lh, ll = split(jnp.concatenate([v_rows, w_rows], axis=0).T)
    rh, rl = split(jnp.concatenate([parts[:, 2560:], parts[:, 2048:2560]], axis=0))
    out[...] = mat[...] - jnp.dot(
        jnp.concatenate([lh, lh, ll], axis=1), jnp.concatenate([rh, rl, rh], axis=0),
        preferred_element_type=F32,
    )
    w_out[...] = w_rows
    v_out[...] = v_rows


def local(mat, pan):
    vmem = pl.BlockSpec(memory_space=pltpu.VMEM)
    parts = pl.pallas_call(
        exchange,
        out_shape=jax.ShapeDtypeStruct((64, 3072), F32),
        in_specs=[pl.BlockSpec(memory_space=pltpu.HBM)] * 2,
        out_specs=vmem,
        scratch_shapes=[
            pltpu.VMEM((1024, 512), F32),
            pltpu.VMEM((64, 1024), F32),
            pltpu.VMEM((32, 128), F32),
            pltpu.VMEM((16, 8, 128), F32),
            pltpu.VMEM((8, 128), F32),
            pltpu.VMEM((4, 8, 128), F32),
            pltpu.VMEM((2, 64, 256), F32),
            pltpu.VMEM((2, 64, 256), F32),
            pltpu.VMEM((16, 8, 256), F32),
            pltpu.VMEM((16, 8, 256), F32),
            pltpu.VMEM((8, 256), F32),
            pltpu.VMEM((8, 256), F32),
            pltpu.VMEM((2, 8, 8, 256), F32),
            pltpu.VMEM((2, 16, 8, 256), F32),
            pltpu.VMEM((4, 128), F32),
            pltpu.VMEM((16, 4, 128), F32),
            pltpu.VMEM((4, 128), F32),
            pltpu.VMEM((32, 4, 128), F32),
            pltpu.SemaphoreType.DMA((11,)),
            pltpu.SemaphoreType.DMA((11,)),
            pltpu.SemaphoreType.DMA((2,)),
            pltpu.SemaphoreType.REGULAR,
        ],
        compiler_params=pltpu.CompilerParams(
            has_side_effects=True, collective_id=0, vmem_limit_bytes=52 * 1024 * 1024
        ),
    )(mat, pan.T)
    across = pl.BlockSpec((64, 512), lambda i: (0, i))
    down = pl.BlockSpec((512, 512), lambda i: (i, 0))
    updated, w_rows, v_rows = pl.pallas_call(
        update,
        grid=(1024 // 512,),
        out_shape=[
            jax.ShapeDtypeStruct((1024, 512), F32),
            jax.ShapeDtypeStruct((64, 1024), F32),
            jax.ShapeDtypeStruct((64, 1024), F32),
        ],
        in_specs=[down, pl.BlockSpec((64, 3072), lambda i: (0, 0))],
        out_specs=[down, across, across],
        compiler_params=pltpu.CompilerParams(vmem_limit_bytes=32 * 1024 * 1024),
    )(mat, parts)
    return updated, w_rows.T, v_rows.T


def solution(mesh):
    return jax.shard_map(
        local,
        mesh=mesh,
        in_specs=(P("row", "col"), P("row", None)),
        out_specs=(P("row", "col"), P("row", None), P("row", None)),
        check_vma=False,
    )
```

```python
import jax
import jax.numpy as jnp
from jax import lax
from jax.experimental import pallas as pl
from jax.experimental.pallas import tpu as pltpu
from jax.sharding import PartitionSpec as P

MESH = pl.DeviceIdType.MESH
HIGH = lax.Precision.HIGHEST
F32 = jnp.float32
BF16 = jnp.bfloat16


def dot(left, right, dims=((1,), (0,))):
    return lax.dot_general(left, right, (dims, ((), ())), precision=HIGH, preferred_element_type=F32)


def split(value):
    high = value.astype(BF16)
    return high, (value - high.astype(F32)).astype(BF16)


def dot3(left, right, dims=((1,), (0,))):
    lh, ll = split(left)
    rh, rl = split(right)

    def one(u, v):
        return lax.dot_general(u, v, (dims, ((), ())), preferred_element_type=F32)

    return one(lh, rh) + (one(lh, rl) + one(ll, rh))


def whole(piece):
    return jnp.concatenate(
        [jnp.concatenate([piece(y, 0), piece(y, 1)], axis=1) for y in range(8)], axis=0
    )


def lower_inverse(gram):
    size = gram.shape[0]
    ids = lax.broadcasted_iota(jnp.int32, (size, 1), 0)
    eye = (
        lax.broadcasted_iota(jnp.int32, (size, size), 0)
        == lax.broadcasted_iota(jnp.int32, (size, size), 1)
    ).astype(F32)
    aug = jnp.concatenate([gram, eye], axis=1)
    for j in range(size):
        row = aug[j : j + 1, :]
        factor = aug[:, j : j + 1] * (1.0 / row[:, j : j + 1])
        aug = aug - jnp.where(ids > j, factor, 0.0) * row
    diag = jnp.sum(aug[:, :size] * eye, axis=1, keepdims=True)
    return aug[:, size:] * lax.rsqrt(diag)


def exchange(
    mat_hbm, pan_hbm, mat, out,
    pan, gsend, grecv, qsend, gall, psend, precv, xsend, xrecv, piece, moved, acol, arow,
    tsend, trecv, usend, urecv,
    ssem, rsem, msem, heard,
):
    r, c = lax.axis_index("row"), lax.axis_index("col")
    y, core, x, z = r // 2, r % 2, c // 8, c % 8
    drains = []

    def put(src, dst, k, row, col, recv=None):
        pltpu.make_async_remote_copy(
            src_ref=src, dst_ref=dst, send_sem=ssem.at[k], recv_sem=rsem.at[k if recv is None else recv],
            device_id={"row": row, "col": col}, device_id_type=MESH,
        ).start()

    def keep(src, dst, k):
        pltpu.make_async_copy(src, dst, rsem.at[k]).start()

    def got(ref, k):
        pltpu.make_async_copy(ref, ref, rsem.at[k]).wait()

    def sent(ref, k):
        drains.append(lambda: pltpu.make_async_copy(ref, ref, ssem.at[k]).wait())

    def loop(first, last, body):
        lax.fori_loop(first, last, lambda i, s: (body(i), s)[1], 0)

    def finish():
        for drain in drains:
            drain()

    barrier = pltpu.get_barrier_semaphore()

    def greet(row, col):
        pl.semaphore_signal(barrier, inc=1, device_id={"row": row, "col": col}, device_id_type=MESH)

    load = pltpu.make_async_copy(mat_hbm, mat, msem.at[0])
    load.start()
    load_pan = pltpu.make_async_copy(pan_hbm, pan, msem.at[1])
    load_pan.start()

    core_to = (x - r // 8) % 2
    x_to = (x - core_to) % 4
    y_to = (z - r % 8 + y + 4) % 8
    half_to = x_to // 2
    row_to, col_to = 2 * y_to + core_to, 8 * x_to + r % 8
    row_up, col_up = c % 16, 8 * ((x + core) % 4) + (z + y - (c % 16) // 2 + 4) % 8
    greet(row_to, col_to)
    greet(row_up, col_up)
    loop(1, 16, lambda i: greet((r + i) % 16, c))
    loop(1, 8, lambda i: greet(r, 8 * x + (z + i) % 8))
    loop(1, 4, lambda i: greet(r, 8 * ((x + i) % 4) + z))

    load_pan.wait()
    for k in range(4):
        low, high = pan[:, 256 * k : 256 * k + 128], pan[:, 256 * k + 128 : 256 * k + 256]
        psend[k // 2, :, 128 * (k % 2) : 128 * (k % 2) + 128] = jnp.where(
            half_to == 0,
            jnp.concatenate([low[:, :64], high[:, :64]], axis=1),
            jnp.concatenate([low[:, 64:], high[:, 64:]], axis=1),
        )
    pant = pan[...]
    gram = dot(pant, pant, ((1,), (1,)))
    gsend[...] = jnp.concatenate([gram[:32], gram[32:]], axis=1)
    load.wait()
    ph, pl_ = split(pant)
    ah, al = split(mat[...])
    both = jnp.dot(jnp.concatenate([ph, pl_], axis=0), ah, preferred_element_type=F32)
    prod = both[:64] + (both[64:] + jnp.dot(ph, al, preferred_element_type=F32))
    for k in range(16):
        xsend[k] = prod[8 * (k // 2) : 8 * (k // 2) + 8, 256 * (k % 2) : 256 * (k % 2) + 256]

    pl.semaphore_wait(barrier, 27)
    put(psend.at[core_to], precv.at[core_to], 0, row_to, col_to)
    sent(psend.at[0], 0)

    def scatter(i):
        d = (r + i) % 16
        put(xsend.at[d], xrecv.at[r], 3, d, c)

    loop(1, 16, scatter)
    keep(xsend.at[r], xrecv.at[r], 3)
    sent(xrecv.at[pl.ds(0, 15)], 3)
    share = gsend.at[pl.ds(pl.multiple_of(8 * x, 8), 8)]
    loop(1, 16, lambda i: put(share, grecv.at[r], 2, (r + i) % 16, c))
    keep(share, grecv.at[r], 2)
    sent(grecv.at[pl.ds(0, 15)], 2)
    loop(1, 4, lambda i: pl.semaphore_signal(
        heard, inc=1, device_id={"row": r, "col": 8 * ((x + i) % 4) + z}, device_id_type=MESH
    ))
    got(xrecv, 3)
    total = xrecv[0]
    for k in range(1, 16):
        total = total + xrecv[k]
    piece[...] = total
    put(piece, moved, 4, row_up, col_up)
    sent(piece, 4)

    got(precv.at[core], 0)
    tpart = dot(total, precv[core], ((1,), (1,)))
    tsend[...] = jnp.concatenate([tpart[:4], tpart[4:]], axis=1)
    me = 2 * z + core

    def share_z(i):
        d = (me + i) % 16
        put(tsend, trecv.at[me], 5, 2 * y + d % 2, 8 * x + d // 2)

    loop(1, 16, share_z)
    keep(tsend, trecv.at[me], 5)
    sent(trecv.at[pl.ds(0, 15)], 5)
    put(precv.at[core], precv.at[core], 1, r + 1 - 2 * core, c)
    sent(precv.at[0], 1)

    got(grecv, 2)
    quarter = grecv[0]
    for k in range(1, 16):
        quarter = quarter + grecv[k]
    qsend[...] = quarter
    loop(1, 4, lambda i: put(qsend, gall.at[x], 8, r, 8 * ((x + i) % 4) + z))
    keep(qsend, gall.at[x], 8)
    sent(gall.at[pl.ds(0, 3)], 8)

    loop(1, 8, lambda i: put(piece, acol.at[core, y], 6, (r + 2 * i) % 16, c))
    keep(piece, acol.at[core, y], 6)
    sent(acol.at[0, pl.ds(0, 7)], 6)

    got(moved, 4)
    pl.semaphore_wait(heard, 3)

    def spread(i):
        d = 8 * (i % 4) + i // 4

        @pl.when(d != c)
        def _():
            put(moved, arow.at[half_to, row_to], 9, r, d)

    loop(0, 32, spread)
    keep(moved, arow.at[half_to, row_to], 9)
    sent(arow.at[0, pl.ds(0, 15)], 9)
    sent(arow.at[1], 9)

    got(trecv, 5)
    total = trecv[0]
    for k in range(1, 16):
        total = total + trecv[k]
    usend[...] = total
    place = 8 * x + y

    def share_xy(i):
        d = (place + i) % 32
        put(usend, urecv.at[place], 7, 2 * (d % 8) + core, 8 * (d // 8) + z)

    loop(1, 32, share_xy)
    keep(usend, urecv.at[place], 7)
    sent(urecv.at[pl.ds(0, 31)], 7)

    got(acol.at[core], 6)
    put(acol.at[core], acol.at[core], 10, r + 1 - 2 * core, c)
    sent(acol.at[0], 10)

    got(gall, 8)
    packed = jnp.concatenate([gall[k] for k in range(4)], axis=0)
    linv = lower_inverse(jnp.concatenate([packed[:, :64], packed[:, 64:]], axis=0))

    v_rows = dot(linv, pant)
    out[:, :1024] = v_rows
    got(precv.at[0], 1)
    v_cols = dot(linv, jnp.concatenate([precv[0], precv[1]], axis=1))
    out[:, 2048:2560] = v_cols
    got(acol.at[0], 10)
    double = 2.0 * linv
    w_cols = dot3(double, whole(lambda y, core: acol[core, y]))
    both = jnp.concatenate([v_rows, v_cols], axis=1)

    got(arow, 9)
    even, odd = (whole(lambda y, core: arow[h, 2 * y + core]) for h in range(2))
    blocks = []
    for k in range(8):
        blocks += [even[:, 64 * k : 64 * k + 64], odd[:, 64 * k : 64 * k + 64]]
    w_rows = dot3(double, jnp.concatenate(blocks, axis=1))

    got(urecv, 7)
    rows = []
    for k in range(8):
        pair = (urecv[k] + urecv[8 + k]) + (urecv[16 + k] + urecv[24 + k])
        rows += [pair[:, :64], pair[:, 64:]]
    corr = dot3(dot3(double, jnp.concatenate(rows, axis=0)), linv, ((1,), (1,)))
    part = dot3(corr, both, ((0,), (0,)))
    out[:, 1024:2048] = w_rows - part[:, :1024]
    out[:, 2560:] = w_cols - part[:, 1024:]
    finish()


def update(mat, parts, out_hbm, w_hbm, v_hbm, out, sems):
    thin = [
        pltpu.make_async_copy(parts.at[:, pl.ds(1024, 1024)], w_hbm, sems.at[0]),
        pltpu.make_async_copy(parts.at[:, pl.ds(0, 1024)], v_hbm, sems.at[1]),
    ]
    for copy in thin:
        copy.start()
    rh, rl = split(jnp.concatenate([parts[:, 2560:], parts[:, 2048:2560]], axis=0))
    right = jnp.concatenate([rh, rl, rh], axis=0)
    copies = []
    for k in range(0, 1024, 256):
        rows = pl.ds(k, 256)
        left = jnp.concatenate([parts[:, k : k + 256], parts[:, 1024 + k : 1024 + k + 256]], axis=0).T
        lh, ll = split(left)
        out[rows, :] = mat[rows, :] - jnp.dot(
            jnp.concatenate([lh, lh, ll], axis=1), right, preferred_element_type=F32
        )
        copies.append(pltpu.make_async_copy(out.at[rows], out_hbm.at[rows], sems.at[2 + k // 256]))
        copies[-1].start()
    for copy in thin + copies:
        copy.wait()


def local(mat, pan):
    vmem = pl.BlockSpec(memory_space=pltpu.VMEM)
    held, parts = pl.pallas_call(
        exchange,
        out_shape=[
            jax.ShapeDtypeStruct((1024, 512), F32),
            jax.ShapeDtypeStruct((64, 3072), F32),
        ],
        in_specs=[pl.BlockSpec(memory_space=pltpu.HBM)] * 2,
        out_specs=[vmem] * 2,
        scratch_shapes=[
            pltpu.VMEM((64, 1024), F32),
            pltpu.VMEM((32, 128), F32),
            pltpu.VMEM((16, 8, 128), F32),
            pltpu.VMEM((8, 128), F32),
            pltpu.VMEM((4, 8, 128), F32),
            pltpu.VMEM((2, 64, 256), F32),
            pltpu.VMEM((2, 64, 256), F32),
            pltpu.VMEM((16, 8, 256), F32),
            pltpu.VMEM((16, 8, 256), F32),
            pltpu.VMEM((8, 256), F32),
            pltpu.VMEM((8, 256), F32),
            pltpu.VMEM((2, 8, 8, 256), F32),
            pltpu.VMEM((2, 16, 8, 256), F32),
            pltpu.VMEM((4, 128), F32),
            pltpu.VMEM((16, 4, 128), F32),
            pltpu.VMEM((4, 128), F32),
            pltpu.VMEM((32, 4, 128), F32),
            pltpu.SemaphoreType.DMA((11,)),
            pltpu.SemaphoreType.DMA((11,)),
            pltpu.SemaphoreType.DMA((2,)),
            pltpu.SemaphoreType.REGULAR,
        ],
        compiler_params=pltpu.CompilerParams(
            has_side_effects=True, collective_id=0, vmem_limit_bytes=50 * 1024 * 1024
        ),
    )(mat, pan.T)
    updated, w_rows, v_rows = pl.pallas_call(
        update,
        out_shape=[
            jax.ShapeDtypeStruct((1024, 512), F32),
            jax.ShapeDtypeStruct((64, 1024), F32),
            jax.ShapeDtypeStruct((64, 1024), F32),
        ],
        in_specs=[vmem] * 2,
        out_specs=[pl.BlockSpec(memory_space=pltpu.HBM)] * 3,
        scratch_shapes=[pltpu.VMEM((1024, 512), F32), pltpu.SemaphoreType.DMA((2 + 1024 // 256,))],
        compiler_params=pltpu.CompilerParams(vmem_limit_bytes=32 * 1024 * 1024),
    )(held, parts)
    return updated, w_rows.T, v_rows.T


def solution(mesh):
    return jax.shard_map(
        local,
        mesh=mesh,
        in_specs=(P("row", "col"), P("row", None)),
        out_specs=(P("row", "col"), P("row", None), P("row", None)),
        check_vma=False,
    )
```

```python
import jax
import jax.numpy as jnp
from jax import lax
from jax.experimental import pallas as pl
from jax.experimental.pallas import tpu as pltpu
from jax.sharding import PartitionSpec as P

MESH = pl.DeviceIdType.MESH
HIGH = lax.Precision.HIGHEST
F32 = jnp.float32
BF16 = jnp.bfloat16


def dot(left, right, dims=((1,), (0,))):
    return lax.dot_general(left, right, (dims, ((), ())), precision=HIGH, preferred_element_type=F32)


def split(value):
    high = value.astype(BF16)
    return high, (value - high.astype(F32)).astype(BF16)


def dot3(left, right, dims=((1,), (0,))):
    lh, ll = split(left)
    rh, rl = split(right)

    def one(u, v):
        return lax.dot_general(u, v, (dims, ((), ())), preferred_element_type=F32)

    return one(lh, rh) + (one(lh, rl) + one(ll, rh))


def whole(piece):
    return jnp.concatenate(
        [jnp.concatenate([piece(y, 0), piece(y, 1)], axis=1) for y in range(8)], axis=0
    )


def lower_inverse(gram):
    size = gram.shape[0]
    ids = lax.broadcasted_iota(jnp.int32, (size, 1), 0)
    eye = (
        lax.broadcasted_iota(jnp.int32, (size, size), 0)
        == lax.broadcasted_iota(jnp.int32, (size, size), 1)
    ).astype(F32)
    aug = jnp.concatenate([gram, eye], axis=1)
    for j in range(size):
        row = aug[j : j + 1, :]
        factor = aug[:, j : j + 1] * (1.0 / row[:, j : j + 1])
        aug = aug - jnp.where(ids > j, factor, 0.0) * row
    diag = jnp.sum(aug[:, :size] * eye, axis=1, keepdims=True)
    return aug[:, size:] * lax.rsqrt(diag)


def exchange(
    mat_hbm, pan, mat, out,
    gsend, grecv, qsend, gall, psend, precv, xsend, xrecv, piece, moved, acol, arow,
    tsend, trecv, usend, urecv,
    ssem, rsem, msem, heard,
):
    r, c = lax.axis_index("row"), lax.axis_index("col")
    y, core, x, z = r // 2, r % 2, c // 8, c % 8
    drains = []

    def put(src, dst, k, row, col, recv=None):
        pltpu.make_async_remote_copy(
            src_ref=src, dst_ref=dst, send_sem=ssem.at[k], recv_sem=rsem.at[k if recv is None else recv],
            device_id={"row": row, "col": col}, device_id_type=MESH,
        ).start()

    def keep(src, dst, k):
        pltpu.make_async_copy(src, dst, rsem.at[k]).start()

    def got(ref, k):
        pltpu.make_async_copy(ref, ref, rsem.at[k]).wait()

    def sent(ref, k):
        drains.append(lambda: pltpu.make_async_copy(ref, ref, ssem.at[k]).wait())

    def loop(first, last, body):
        lax.fori_loop(first, last, lambda i, s: (body(i), s)[1], 0)

    def finish():
        for drain in drains:
            drain()

    barrier = pltpu.get_barrier_semaphore()

    def greet(row, col):
        pl.semaphore_signal(barrier, inc=1, device_id={"row": row, "col": col}, device_id_type=MESH)

    load = pltpu.make_async_copy(mat_hbm, mat, msem.at[0])
    load.start()

    core_to = (x - r // 8) % 2
    x_to = (x - core_to) % 4
    y_to = (z - r % 8 + y + 4) % 8
    half_to = x_to // 2
    row_to, col_to = 2 * y_to + core_to, 8 * x_to + r % 8
    row_up, col_up = c % 16, 8 * ((x + core) % 4) + (z + y - (c % 16) // 2 + 4) % 8
    greet(row_to, col_to)
    greet(row_up, col_up)
    loop(1, 16, lambda i: greet((r + i) % 16, c))
    loop(1, 8, lambda i: greet(r, 8 * x + (z + i) % 8))
    loop(1, 4, lambda i: greet(r, 8 * ((x + i) % 4) + z))

    for k in range(4):
        low, high = pan[:, 256 * k : 256 * k + 128], pan[:, 256 * k + 128 : 256 * k + 256]
        psend[k // 2, :, 128 * (k % 2) : 128 * (k % 2) + 128] = jnp.where(
            half_to == 0,
            jnp.concatenate([low[:, :64], high[:, :64]], axis=1),
            jnp.concatenate([low[:, 64:], high[:, 64:]], axis=1),
        )
    pant = pan[...]
    gram = dot(pant, pant, ((1,), (1,)))
    gsend[...] = jnp.concatenate([gram[:32], gram[32:]], axis=1)
    load.wait()
    ph, pl_ = split(pant)
    ah, al = split(mat[...])
    both = jnp.dot(jnp.concatenate([ph, pl_], axis=0), ah, preferred_element_type=F32)
    prod = both[:64] + (both[64:] + jnp.dot(ph, al, preferred_element_type=F32))
    for k in range(16):
        xsend[k] = prod[8 * (k // 2) : 8 * (k // 2) + 8, 256 * (k % 2) : 256 * (k % 2) + 256]

    pl.semaphore_wait(barrier, 27)
    put(psend.at[core_to, pl.ds(0, 32)], precv.at[core_to, pl.ds(0, 32)], 0, row_to, col_to)
    put(psend.at[core_to, pl.ds(32, 32)], precv.at[core_to, pl.ds(32, 32)], 11, row_to, col_to)
    sent(psend.at[0, pl.ds(0, 32)], 0)
    sent(psend.at[0, pl.ds(0, 32)], 11)

    def scatter(i):
        d = (r + i) % 16
        put(xsend.at[d], xrecv.at[r], 3, d, c)

    loop(1, 16, scatter)
    keep(xsend.at[r], xrecv.at[r], 3)
    sent(xrecv.at[pl.ds(0, 15)], 3)
    share = gsend.at[pl.ds(pl.multiple_of(8 * x, 8), 8)]
    loop(1, 16, lambda i: put(share, grecv.at[r], 2, (r + i) % 16, c))
    keep(share, grecv.at[r], 2)
    sent(grecv.at[pl.ds(0, 15)], 2)
    loop(1, 4, lambda i: pl.semaphore_signal(
        heard, inc=1, device_id={"row": r, "col": 8 * ((x + i) % 4) + z}, device_id_type=MESH
    ))
    got(xrecv, 3)
    total = xrecv[0]
    for k in range(1, 16):
        total = total + xrecv[k]
    piece[...] = total
    put(piece, moved, 4, row_up, col_up)
    sent(piece, 4)

    got(precv.at[core, pl.ds(0, 32)], 0)
    got(precv.at[core, pl.ds(0, 32)], 11)
    tpart = dot3(total, precv[core], ((1,), (1,)))
    tsend[...] = jnp.concatenate([tpart[:4], tpart[4:]], axis=1)
    me = 2 * z + core

    def share_z(i):
        d = (me + i) % 16
        put(tsend, trecv.at[me], 5, 2 * y + d % 2, 8 * x + d // 2)

    loop(1, 16, share_z)
    keep(tsend, trecv.at[me], 5)
    sent(trecv.at[pl.ds(0, 15)], 5)
    put(precv.at[core], precv.at[core], 1, r + 1 - 2 * core, c)
    sent(precv.at[0], 1)

    got(grecv, 2)
    quarter = grecv[0]
    for k in range(1, 16):
        quarter = quarter + grecv[k]
    qsend[...] = quarter
    loop(1, 4, lambda i: put(qsend, gall.at[x], 8, r, 8 * ((x + i) % 4) + z))
    keep(qsend, gall.at[x], 8)
    sent(gall.at[pl.ds(0, 3)], 8)

    loop(1, 8, lambda i: put(piece, acol.at[core, y], 6, (r + 2 * i) % 16, c))
    keep(piece, acol.at[core, y], 6)
    sent(acol.at[0, pl.ds(0, 7)], 6)

    got(moved, 4)
    pl.semaphore_wait(heard, 3)

    def spread(i):
        d = 8 * (i % 4) + i // 4

        @pl.when(d != c)
        def _():
            put(moved, arow.at[half_to, row_to], 9, r, d)

    loop(0, 32, spread)
    keep(moved, arow.at[half_to, row_to], 9)
    sent(arow.at[0, pl.ds(0, 15)], 9)
    sent(arow.at[1], 9)

    got(trecv, 5)
    total = trecv[0]
    for k in range(1, 16):
        total = total + trecv[k]
    usend[...] = total
    place = 8 * x + y

    def share_xy(i):
        d = (place + i) % 32
        put(usend, urecv.at[place], 7, 2 * (d % 8) + core, 8 * (d // 8) + z)

    loop(1, 32, share_xy)
    keep(usend, urecv.at[place], 7)
    sent(urecv.at[pl.ds(0, 31)], 7)

    got(acol.at[core], 6)
    put(acol.at[core], acol.at[core], 10, r + 1 - 2 * core, c)
    sent(acol.at[0], 10)

    got(gall, 8)
    packed = jnp.concatenate([gall[k] for k in range(4)], axis=0)
    linv = lower_inverse(jnp.concatenate([packed[:, :64], packed[:, 64:]], axis=0))

    v_rows = dot(linv, pant)
    out[:, :1024] = v_rows
    got(precv.at[0], 1)
    v_cols = dot(linv, jnp.concatenate([precv[0], precv[1]], axis=1))
    out[:, 2048:2560] = v_cols
    got(acol.at[0], 10)
    double = 2.0 * linv
    w_cols = dot3(double, whole(lambda y, core: acol[core, y]))
    both = jnp.concatenate([v_rows, v_cols], axis=1)

    finish()
    got(arow, 9)
    even, odd = (whole(lambda y, core: arow[h, 2 * y + core]) for h in range(2))
    blocks = []
    for k in range(8):
        blocks += [even[:, 64 * k : 64 * k + 64], odd[:, 64 * k : 64 * k + 64]]
    w_rows = dot3(double, jnp.concatenate(blocks, axis=1))

    got(urecv, 7)
    rows = []
    for k in range(8):
        pair = (urecv[k] + urecv[8 + k]) + (urecv[16 + k] + urecv[24 + k])
        rows += [pair[:, :64], pair[:, 64:]]
    corr = dot3(dot3(double, jnp.concatenate(rows, axis=0)), linv, ((1,), (1,)))
    part = dot3(corr, both, ((0,), (0,)))
    out[:, 1024:2048] = w_rows - part[:, :1024]
    out[:, 2560:] = w_cols - part[:, 1024:]


def update(mat, parts, out_hbm, w_hbm, v_hbm, out, sems):
    thin = [
        pltpu.make_async_copy(parts.at[:, pl.ds(1024, 1024)], w_hbm, sems.at[0]),
        pltpu.make_async_copy(parts.at[:, pl.ds(0, 1024)], v_hbm, sems.at[1]),
    ]
    for copy in thin:
        copy.start()
    rh, rl = split(jnp.concatenate([parts[:, 2560:], parts[:, 2048:2560]], axis=0))
    right = jnp.concatenate([rh, rl, rh], axis=0)
    copies = []
    for k in range(0, 1024, 256):
        rows = pl.ds(k, 256)
        left = jnp.concatenate([parts[:, k : k + 256], parts[:, 1024 + k : 1024 + k + 256]], axis=0).T
        lh, ll = split(left)
        out[rows, :] = mat[rows, :] - jnp.dot(
            jnp.concatenate([lh, lh, ll], axis=1), right, preferred_element_type=F32
        )
        copies.append(pltpu.make_async_copy(out.at[rows], out_hbm.at[rows], sems.at[2 + k // 256]))
        copies[-1].start()
    for copy in thin + copies:
        copy.wait()


def local(mat, pan):
    vmem = pl.BlockSpec(memory_space=pltpu.VMEM)
    held, parts = pl.pallas_call(
        exchange,
        out_shape=[
            jax.ShapeDtypeStruct((1024, 512), F32),
            jax.ShapeDtypeStruct((64, 3072), F32),
        ],
        in_specs=[pl.BlockSpec(memory_space=pltpu.HBM), vmem],
        out_specs=[vmem] * 2,
        scratch_shapes=[
            pltpu.VMEM((32, 128), F32),
            pltpu.VMEM((16, 8, 128), F32),
            pltpu.VMEM((8, 128), F32),
            pltpu.VMEM((4, 8, 128), F32),
            pltpu.VMEM((2, 64, 256), F32),
            pltpu.VMEM((2, 64, 256), F32),
            pltpu.VMEM((16, 8, 256), F32),
            pltpu.VMEM((16, 8, 256), F32),
            pltpu.VMEM((8, 256), F32),
            pltpu.VMEM((8, 256), F32),
            pltpu.VMEM((2, 8, 8, 256), F32),
            pltpu.VMEM((2, 16, 8, 256), F32),
            pltpu.VMEM((4, 128), F32),
            pltpu.VMEM((16, 4, 128), F32),
            pltpu.VMEM((4, 128), F32),
            pltpu.VMEM((32, 4, 128), F32),
            pltpu.SemaphoreType.DMA((12,)),
            pltpu.SemaphoreType.DMA((12,)),
            pltpu.SemaphoreType.DMA((2,)),
            pltpu.SemaphoreType.REGULAR,
        ],
        compiler_params=pltpu.CompilerParams(
            has_side_effects=True, collective_id=0, vmem_limit_bytes=50 * 1024 * 1024
        ),
    )(mat, pan.T)
    updated, w_rows, v_rows = pl.pallas_call(
        update,
        out_shape=[
            jax.ShapeDtypeStruct((1024, 512), F32),
            jax.ShapeDtypeStruct((64, 1024), F32),
            jax.ShapeDtypeStruct((64, 1024), F32),
        ],
        in_specs=[vmem] * 2,
        out_specs=[pl.BlockSpec(memory_space=pltpu.HBM)] * 3,
        scratch_shapes=[pltpu.VMEM((1024, 512), F32), pltpu.SemaphoreType.DMA((2 + 1024 // 256,))],
        compiler_params=pltpu.CompilerParams(vmem_limit_bytes=32 * 1024 * 1024),
    )(held, parts)
    return updated, w_rows.T, v_rows.T


def solution(mesh):
    return jax.shard_map(
        local,
        mesh=mesh,
        in_specs=(P("row", "col"), P("row", None)),
        out_specs=(P("row", "col"), P("row", None), P("row", None)),
        check_vma=False,
    )
```
